256 devices in a mesh: energy: 8 (over z), atom: 32 (over x, y, core).
Axes of the slice: x: 4, y: 4, z: 8, core: 2. Of those that a mesh axis runs over, the one named last changes fastest.
Arguments:
- t_mats: bfloat16 [8, 64, 2048], P('energy', 'atom'), may hold values from -0.75 to 0.75
- struct_table: bfloat16 [8, 64, 2048], P('energy'), may hold values from -0.359375 to 0.359375
- zone_atoms: int32 [64, 64], P('atom'), may hold values from 0 to 63, as said below
- zone_size: int32 [64], P('atom'), may hold values from 32 to 64
- pair_index: int32 [64, 384], P('atom'), may hold values from 0 to 63
- zone_link: int32 [64, 384], P('atom'), may hold values from 0 to 63
- weights: float32 [8, 2], P('energy'), may hold values from -1 to 1
Outputs:
- green: float32 [64, 2048], P('atom')
The draws below stay inside these ranges and needn't reach their ends.
Inputs may be any that keep to these rules, and one draw needn't show every extreme that they name: Atom g is owned by index g // 2 of the atom axis; zone_atoms[g, 0] is g; the owner of every member of atom g's zone lies -16 to 15 steps from g's owner along the atom axis, counted around the axis, and both extreme offsets occur in every zone; members may repeat (periodic images).
All inputs are finite; a program needn't handle non-finite values.
Results may differ from the reference program's by a relative error of at most 0.003.
Values may be sent and summed in bfloat16 or wider, within the bound.
A program may use at most 128 MiB of HBM per device.

```python
import jax
import jax.numpy as jnp
from jax import lax

L = 32
Z = 64
NB = 6
KTAB = 64
ITERS = 3
A_DEV = 2
ATOMS = 64
NE = 8
REACH = 16


def draw_zone_atoms(key, part):
    key_offset, key_local = jax.random.split(jax.random.fold_in(key, 7))
    owners_total = ATOMS // A_DEV
    offsets = jax.random.randint(key_offset, (ATOMS, Z), -REACH, REACH)
    offsets = offsets.at[:, 1].set(REACH - 1).at[:, 2].set(-REACH)
    local_ids = jax.random.randint(key_local, (ATOMS, Z), 0, A_DEV)
    owner_ids = jnp.arange(ATOMS, dtype=jnp.int32) // A_DEV
    member_ids = (owner_ids[:, None] + offsets) % owners_total * A_DEV + local_ids
    member_ids = member_ids.at[:, 0].set(jnp.arange(ATOMS, dtype=jnp.int32))
    return member_ids.astype(jnp.int32)


def plant(array, key, low, largest):
    longest = array.shape.index(max(array.shape))
    spots = []
    for shift in (0, 1):
        where = [jax.random.randint(jax.random.fold_in(key, axis), (), 0, length) for axis, length in enumerate(array.shape)]
        where[longest] = (where[longest] + shift) % array.shape[longest]
        spots.append(tuple(where))
    return array.at[spots[0]].set(low).at[spots[1]].set(largest)


def block_scale(own_key, extent, pieces, low, top_value):
    factor_of = 1.0
    for axis_at, blocks in pieces:
        steps = jax.random.uniform(jax.random.fold_in(jax.random.fold_in(own_key, 6), axis_at), (blocks,), jnp.float32, low / len(pieces), top_value / len(pieces))
        factor_of = factor_of * jnp.repeat(jnp.exp(steps), extent[axis_at] // blocks).reshape((-1,) + (1,) * (len(extent) - 1 - axis_at))
    return factor_of


def scatter_about(own_key, extent, deviation, most, cuts=(), kind=jnp.bfloat16):
    result = jax.random.normal(own_key, extent, jnp.float32) * deviation
    if len(cuts) > 0:
        result = block_scale(own_key, extent, cuts, -0.22, 0.18) * result
    return jnp.clip(result, min=-most, max=most).astype(kind)


def setup_inputs(seed: int = 0) -> dict:
    key_list = jax.random.split(jax.random.key(seed), 8)
    return {
        "t_mats": scatter_about(key_list[0], (NE, ATOMS, 2 * L * L), 0.125, 0.75, ((0, 8), (1, 32))),
        "struct_table": scatter_about(key_list[1], (NE, KTAB, 2 * L * L), 0.06, 0.359375, ((0, 8),)),
        "zone_atoms": draw_zone_atoms(jax.random.fold_in(key_list[7], 71), 0),
        "zone_size": plant(jax.random.randint(key_list[3], (ATOMS,), Z // 2, Z + 1), jax.random.fold_in(key_list[3], 1), Z // 2, Z).astype(jnp.int32),
        "pair_index": plant(jax.random.randint(key_list[4], (ATOMS, Z * NB), 0, KTAB), jax.random.fold_in(key_list[4], 1), 0, KTAB - 1).astype(jnp.int32),
        "zone_link": plant(jax.random.randint(key_list[5], (ATOMS, Z * NB), 0, Z), jax.random.fold_in(key_list[5], 1), 0, Z - 1).astype(jnp.int32),
        "weights": jnp.clip(jax.random.uniform(key_list[6], (NE, 2), jnp.float32, -1.0, 1.0) * block_scale(key_list[6], (NE, 2), ((0, 8),), -0.4, 0.0), -1.0, 1.0),
    }


def real_form(block):
    parts = block.reshape(block.shape[:-1] + (2, L, L))
    real_part = parts[..., 0, :, :]
    imag_part = parts[..., 1, :, :]
    top_rows = jnp.concatenate([real_part, -imag_part], axis=-1)
    bottom_rows = jnp.concatenate([imag_part, real_part], axis=-1)
    return jnp.concatenate([top_rows, bottom_rows], axis=-2)


def solve_zone(zone_block, table_real, pairs, links):
    t_real = real_form(zone_block).astype(jnp.float32)
    couplings = table_real[pairs.reshape(Z, NB)].astype(jnp.float32)
    link_table = links.reshape(Z, NB)
    start = jnp.zeros((Z, 2 * L, L), jnp.float32).at[0].set(t_real[0, :, :L])
    column = start
    for repeat in range(ITERS):
        near = column.astype(jnp.bfloat16).astype(jnp.float32)[link_table]
        coupled = jnp.einsum("anij,anjk->aik", couplings, near, precision=lax.Precision.HIGHEST)
        coupled = coupled.astype(jnp.bfloat16).astype(jnp.float32)
        column = jnp.einsum("aij,ajk->aik", t_real, coupled, precision=lax.Precision.HIGHEST) + start
    return column[0]


def reference(t_mats, struct_table, zone_atoms, zone_size, pair_index, zone_link, weights):
    present = jnp.arange(Z, dtype=jnp.int32)[None, :] < zone_size[:, None]

    def one_energy(inputs):
        t_energy, table_energy = inputs
        table_real = real_form(table_energy)

        def one_atom(atom_inputs):
            members, keep, pairs, links = atom_inputs
            zone_block = jnp.where(keep[:, None], t_energy[members], jnp.zeros((), jnp.bfloat16))
            return solve_zone(zone_block, table_real, pairs, links)

        return lax.map(one_atom, (zone_atoms, present, pair_index, zone_link))

    diagonal = lax.map(one_energy, (t_mats, struct_table))
    real_rows = diagonal[:, :, :L, :].reshape(NE, ATOMS, L * L)
    imag_rows = diagonal[:, :, L:, :].reshape(NE, ATOMS, L * L)
    w_real = weights[:, 0][:, None, None]
    w_imag = weights[:, 1][:, None, None]
    green_real = jnp.sum(w_real * real_rows - w_imag * imag_rows, axis=0)
    green_imag = jnp.sum(w_real * imag_rows + w_imag * real_rows, axis=0)
    return jnp.concatenate([green_real, green_imag], axis=-1)
```

```python
import functools

import jax
import jax.numpy as jnp
from jax import lax
from jax.experimental import pallas as pl
from jax.experimental.pallas import tpu as pltpu
from jax.sharding import PartitionSpec as P

L = 32
Z = 64
NB = 6
KTAB = 64
ROWS = 16
LANES = 128
FORM = 64
MESH = pl.DeviceIdType.MESH
NT = (((1,), (1,)), ((), ()))


def iota2(shape, dim):
    return lax.broadcasted_iota(jnp.int32, shape, dim)


def dot_nt(a, b):
    return lax.dot_general(a, b, NT, preferred_element_type=jnp.float32)


def dot(a, b):
    return jnp.dot(a, b, preferred_element_type=jnp.float32)


def to_bf16_mask(cond):
    return jnp.where(cond, 1.0, 0.0).astype(jnp.bfloat16)


def form_matrix():
    i = iota2((256, 512), 0)
    j = iota2((256, 512), 1)
    h, s1, c = i >> 7, (i >> 5) & 3, i & 31
    s, l = j >> 7, j & 127
    return to_bf16_mask(
        (s1 == s) & (l < 64) & (((l >> 3) & 1) == h) & (((l & 7) * 4 + (l >> 4)) == c)
    )


def spread_matrix():
    i = iota2((64, 256), 0)
    j = iota2((64, 256), 1)
    return to_bf16_mask(
        (((i >> 3) & 1) == (j >> 7)) & (((i & 7) * 4 + (i >> 4)) == (j & 31))
    )


def start_matrix():
    k = iota2((L, FORM), 0)
    l = iota2((L, FORM), 1)
    return to_bf16_mask((((l >> 3) & 1) == 0) & (((l & 7) * 4 + (l >> 4)) == k))


def partner(x):
    n = x.shape[0] // ROWS
    halves = x.reshape(n, 2, 8, LANES)
    return jnp.concatenate([-halves[:, 1:], halves[:, :1]], axis=1).reshape(n * ROWS, LANES)


def with_partner(x32):
    return jnp.concatenate(
        [x32.astype(jnp.bfloat16), partner(x32).astype(jnp.bfloat16)], axis=1
    )


def kernel(
    ne, na, adev,
    t_hbm, tab_hbm, atoms_hbm, size_hbm, pair_hbm, link_hbm, w_hbm,
    out_ref,
    t_ref, tab_ref, atoms, size, pair, link, w_ref,
    xf, gath, tabx, gform, tform, pbuf, c1, c1rep, near, arbuf,
    in_sems, ag_send, ag_recv, ar_send, ar_recv,
):
    e = lax.axis_index("energy")
    me = lax.axis_index("atom")
    n_atoms = na * adev
    blk = adev * ROWS

    sources = (t_hbm, tab_hbm, link_hbm, pair_hbm, atoms_hbm, size_hbm, w_hbm)
    landed = (t_ref, tab_ref, link, pair, atoms, size, w_ref)
    loads = [
        pltpu.make_async_copy(src, dst, in_sems.at[i])
        for i, (src, dst) in enumerate(zip(sources, landed))
    ]
    for copy in loads:
        copy.start()

    barrier = pltpu.get_barrier_semaphore()

    def greet_atom(d, _):
        pl.semaphore_signal(
            barrier, inc=1, device_id=(e, lax.rem(me + d, na)), device_id_type=MESH
        )
        return 0

    def greet_energy(d, _):
        pl.semaphore_signal(
            barrier, inc=1, device_id=(lax.rem(e + d, ne), me), device_id_type=MESH
        )
        return 0

    lax.fori_loop(1, na, greet_atom, 0)
    lax.fori_loop(1, ne, greet_energy, 0)

    loads[0].wait()
    for t in range(ROWS):
        xf[pl.ds(t, adev, stride=ROWS), :] = t_ref[
            0, :, t * LANES : (t + 1) * LANES
        ].astype(jnp.float32)
    own32 = xf[...]
    own = own32.astype(jnp.bfloat16)
    my_rows = pl.ds(me * adev, adev)
    for z in range(adev):
        gath[me * adev + z] = own[z * ROWS : (z + 1) * ROWS]
    gath[n_atoms] = jnp.zeros((ROWS, LANES), jnp.bfloat16)

    pl.semaphore_wait(barrier, na - 1 + ne - 1)

    def send(d, _):
        pltpu.make_async_remote_copy(
            src_ref=gath.at[my_rows],
            dst_ref=gath.at[my_rows],
            send_sem=ag_send,
            recv_sem=ag_recv,
            device_id=(e, lax.rem(me + d, na)),
            device_id_type=MESH,
        ).start()
        return 0

    lax.fori_loop(1, na, send, 0)

    ab = form_matrix()
    loads[1].wait()
    for t in range(ROWS):
        tabx[pl.ds(t, KTAB, stride=ROWS), :] = tab_ref[
            0, :, t * LANES : (t + 1) * LANES
        ].astype(jnp.float32)

    def put_forms(dst, first, lhs):
        forms = dot(lhs, ab).astype(jnp.bfloat16)
        for k in range(lhs.shape[0] // ROWS):
            for s in range(4):
                dst[first + k, s * ROWS : (s + 1) * ROWS, :] = forms[
                    k * ROWS : (k + 1) * ROWS, s * LANES : (s + 1) * LANES
                ]

    def table_forms(i, _):
        rows = tabx[pl.ds(pl.multiple_of(i * 128, 128), 128), :]
        put_forms(gform, i * 8, with_partner(rows))
        return 0

    lax.fori_loop(0, KTAB // 8, table_forms, 0)
    put_forms(tform, 0, with_partner(own32))

    def form(ref, k):
        return ref[k][:, :FORM]

    sel = start_matrix()
    start = [dot_nt(sel, form(tform, z)) for z in range(adev)]
    start_all = jnp.concatenate(start, axis=0).astype(jnp.bfloat16)

    def table_times_start(i, _):
        for k in range(8):
            b = i * 8 + k
            term = dot_nt(start_all, form(gform, b))
            for z in range(adev):
                pbuf[z, b] = term[z * L : (z + 1) * L]
        return 0

    lax.fori_loop(0, KTAB // 8, table_times_start, 0)
    for z in range(adev):
        pbuf[z, KTAB] = jnp.zeros((L, FORM), jnp.float32)

    slots = NB * NB
    for copy in loads[2:]:
        copy.wait()
    for z in range(adev):

        def first_coupled(n, _, z=z):
            b = link[z, n]
            for m in range(NB):
                a = link[z, b * NB + m]
                acc = None
                for j in range(NB):
                    at = a * NB + j
                    term = pbuf[z, jnp.minimum(pair[z, at] + link[z, at] * KTAB, KTAB)]
                    acc = term if acc is None else acc + term
                c1[pl.ds(pl.multiple_of((z * slots + n * NB + m) * L, L), L), :] = acc.astype(
                    jnp.bfloat16
                )
            return 0

        lax.fori_loop(0, NB, first_coupled, 0)

    rep = spread_matrix()

    def spread(i, _):
        rows = pl.ds(pl.multiple_of(i * 256, 256), 256)
        c1rep[rows, :] = dot(c1[rows, :], rep).astype(jnp.bfloat16)
        return 0

    lax.fori_loop(0, adev * slots * L // 256, spread, 0)

    others = gath.at[pl.ds(0, (na - 1) * adev)]
    pltpu.make_async_copy(others, others, ag_recv).wait()
    pltpu.make_async_copy(others, others, ag_send).wait()

    lane_group = iota2((ROWS, LANES), 1) >> 5

    def member(z, a):
        absent = jnp.maximum(a - size[z] + 1, 0)
        return jnp.minimum(atoms[z, a] + absent * n_atoms, n_atoms)

    def is_first(a):
        return 1.0 - jnp.minimum(a, 1).astype(jnp.float32)

    def packed(atom):
        return gath[atom]

    def wide_form(x):
        x32 = x.astype(jnp.float32)
        y32 = jnp.concatenate([-x32[8:], x32[:8]], axis=0)

        def groups(v):
            return jnp.concatenate(
                [jnp.where(lane_group == s, v, 0.0).astype(jnp.bfloat16) for s in range(4)],
                axis=0,
            )

        return jnp.concatenate([groups(x32), groups(y32)], axis=1)

    for z in range(adev):
        x32 = jnp.concatenate(
            [packed(member(z, link[z, n])) for n in range(NB)], axis=0
        ).astype(jnp.float32)
        put_forms(tform, adev + z * NB, with_partner(x32))

    for z in range(adev):

        def first_column(n, _, z=z):
            b = link[z, n]
            for m in range(NB):
                a = link[z, b * NB + m]
                at = pl.ds(pl.multiple_of((z * slots + n * NB + m) * L, L), L)
                col = dot_nt(c1rep[at, :], wide_form(packed(member(z, a))))
                col = col + is_first(a) * start[z]
                near[at, :] = col.astype(jnp.bfloat16)
            return 0

        lax.fori_loop(0, NB, first_column, 0)

    lane_group_f = iota2((ROWS, LANES), 1) >> 5
    w_re = w_ref[0, 0]
    w_im = w_ref[0, 1]
    mine = pl.multiple_of(e * blk, blk)
    for z in range(adev):
        total = None
        for n in range(NB):
            b = link[z, n]
            acc = None
            for m in range(NB):
                at = (z * slots + n * NB + m) * L
                term = dot_nt(near[at : at + L, :], form(gform, pair[z, b * NB + m]))
                acc = term if acc is None else acc + term
            col = dot_nt(acc.astype(jnp.bfloat16), form(tform, adev + z * NB + n))
            col = col + is_first(b) * start[z]
            term = dot_nt(col.astype(jnp.bfloat16), form(gform, pair[z, n]))
            total = term if total is None else total + term
        coupled = total.astype(jnp.bfloat16)
        diag = dot_nt(form(tform, z), jnp.concatenate([coupled] * 4, axis=0))
        block = xf[z * ROWS : (z + 1) * ROWS, :]
        for s in range(4):
            block = block + jnp.where(
                lane_group_f == s, diag[s * ROWS : (s + 1) * ROWS, :], 0.0
            )
        re, im = block[:8], block[8:]
        arbuf[pl.ds(mine + z * ROWS, 8), :] = w_re * re - w_im * im
        arbuf[pl.ds(mine + z * ROWS + 8, 8), :] = w_re * im + w_im * re

    def share(d, _):
        pltpu.make_async_remote_copy(
            src_ref=arbuf.at[pl.ds(mine, blk)],
            dst_ref=arbuf.at[pl.ds(mine, blk)],
            send_sem=ar_send,
            recv_sem=ar_recv,
            device_id=(lax.rem(e + d, ne), me),
            device_id_type=MESH,
        ).start()
        return 0

    lax.fori_loop(1, ne, share, 0)
    rest = arbuf.at[pl.ds(0, (ne - 1) * blk)]
    pltpu.make_async_copy(rest, rest, ar_recv).wait()
    pltpu.make_async_copy(rest, rest, ar_send).wait()
    green = arbuf[0:blk, :]
    for i in range(1, ne):
        green = green + arbuf[i * blk : (i + 1) * blk, :]
    out_ref[...] = green


def body(t_mats, struct_table, zone_atoms, zone_size, pair_index, zone_link, weights, ne, na):
    adev = t_mats.shape[1]
    slots = NB * NB
    given = (t_mats, struct_table, zone_atoms, zone_size, pair_index, zone_link, weights)
    bf16, f32 = jnp.bfloat16, jnp.float32
    green = pl.pallas_call(
        functools.partial(kernel, ne, na, adev),
        out_shape=jax.ShapeDtypeStruct((adev * ROWS, LANES), f32),
        in_specs=[pl.BlockSpec(memory_space=pltpu.HBM)] * len(given),
        out_specs=pl.BlockSpec(memory_space=pltpu.VMEM),
        scratch_shapes=[
            *[pltpu.VMEM(a.shape, a.dtype) for a in given[:2]],
            *[pltpu.SMEM(a.shape, a.dtype) for a in given[2:]],
            pltpu.VMEM((adev * ROWS, LANES), f32),
            pltpu.VMEM((na * adev + 1, ROWS, LANES), bf16),
            pltpu.VMEM((KTAB * ROWS, LANES), f32),
            pltpu.VMEM((KTAB, FORM, LANES), bf16),
            pltpu.VMEM((adev * (1 + NB), FORM, LANES), bf16),
            pltpu.VMEM((adev, KTAB + 1, L, FORM), f32),
            pltpu.VMEM((adev * slots * L, FORM), bf16),
            pltpu.VMEM((adev * slots * L, 256), bf16),
            pltpu.VMEM((adev * slots * L, FORM), bf16),
            pltpu.VMEM((ne * adev * ROWS, LANES), f32),
            pltpu.SemaphoreType.DMA((len(given),)),
            pltpu.SemaphoreType.DMA,
            pltpu.SemaphoreType.DMA,
            pltpu.SemaphoreType.DMA,
            pltpu.SemaphoreType.DMA,
        ],
        compiler_params=pltpu.CompilerParams(
            collective_id=0, has_side_effects=True, vmem_limit_bytes=32 * 1024 * 1024
        ),
    )(*given)
    return green.reshape(adev, 2 * L * L)


def solution(mesh):
    ne, na = mesh.shape["energy"], mesh.shape["atom"]
    return jax.shard_map(
        functools.partial(body, ne=ne, na=na),
        mesh=mesh,
        in_specs=(
            P("energy", "atom", None),
            P("energy", None, None),
            P("atom", None),
            P("atom"),
            P("atom", None),
            P("atom", None),
            P("energy", None),
        ),
        out_specs=P("atom", None),
        check_vma=False,
    )
```

```python
import functools

import jax
import jax.numpy as jnp
from jax import lax
from jax.experimental import pallas as pl
from jax.experimental.pallas import tpu as pltpu
from jax.sharding import PartitionSpec as P

L = 32
Z = 64
NB = 6
KTAB = 64
ROWS = 16
LANES = 128
FORM = 64
MESH = pl.DeviceIdType.MESH
NT = (((1,), (1,)), ((), ()))


def iota2(shape, dim):
    return lax.broadcasted_iota(jnp.int32, shape, dim)


def dot_nt(a, b):
    return lax.dot_general(a, b, NT, preferred_element_type=jnp.float32)


def dot(a, b):
    return jnp.dot(a, b, preferred_element_type=jnp.float32)


def to_bf16_mask(cond):
    return jnp.where(cond, 1.0, 0.0).astype(jnp.bfloat16)


def form_matrix():
    i = iota2((256, 512), 0)
    j = iota2((256, 512), 1)
    h, s1, c = i >> 7, (i >> 5) & 3, i & 31
    s, l = j >> 7, j & 127
    return to_bf16_mask(
        (s1 == s) & (l < 64) & (((l >> 3) & 1) == h) & (((l & 7) * 4 + (l >> 4)) == c)
    )


def start_matrix():
    k = iota2((L, LANES), 0)
    l = iota2((L, LANES), 1)
    return to_bf16_mask(
        (l < FORM) & (((l >> 3) & 1) == 0) & (((l & 7) * 4 + (l >> 4)) == k)
    )


def partner(x):
    n = x.shape[0] // ROWS
    halves = x.reshape(n, 2, 8, LANES)
    return jnp.concatenate([-halves[:, 1:], halves[:, :1]], axis=1).reshape(n * ROWS, LANES)


def with_partner(x32):
    return jnp.concatenate(
        [x32.astype(jnp.bfloat16), partner(x32).astype(jnp.bfloat16)], axis=1
    )


def kernel(
    ne, na, adev,
    t_hbm, tab_hbm, atoms_hbm, size_hbm, pair_hbm, link_hbm, w_hbm,
    out_ref,
    t_ref, tab_ref, atoms, size, pair, link, w_ref,
    xf, gath, tabx, gform, own_form, tform, pbuf, c1, near1, near2, wide, arbuf,
    in_sems, ag_send, ag_recv, ar_send, ar_recv,
):
    e = lax.axis_index("energy")
    me = lax.axis_index("atom")
    n_atoms = na * adev
    blk = adev * ROWS

    sources = (t_hbm, tab_hbm, link_hbm, pair_hbm, atoms_hbm, size_hbm, w_hbm)
    landed = (t_ref, tab_ref, link, pair, atoms, size, w_ref)
    loads = [
        pltpu.make_async_copy(src, dst, in_sems.at[i])
        for i, (src, dst) in enumerate(zip(sources, landed))
    ]
    for copy in loads:
        copy.start()

    barrier = pltpu.get_barrier_semaphore()

    def greet_atom(d, _):
        pl.semaphore_signal(
            barrier, inc=1, device_id=(e, lax.rem(me + d, na)), device_id_type=MESH
        )
        return 0

    def greet_energy(d, _):
        pl.semaphore_signal(
            barrier, inc=1, device_id=(lax.rem(e + d, ne), me), device_id_type=MESH
        )
        return 0

    lax.fori_loop(1, na, greet_atom, 0)
    lax.fori_loop(1, ne, greet_energy, 0)

    loads[0].wait()
    for t in range(ROWS):
        xf[pl.ds(t, adev, stride=ROWS), :] = t_ref[
            0, :, t * LANES : (t + 1) * LANES
        ].astype(jnp.float32)
    own32 = xf[...]
    own = own32.astype(jnp.bfloat16)
    my_rows = pl.ds(me * adev, adev)
    for z in range(adev):
        gath[me * adev + z] = own[z * ROWS : (z + 1) * ROWS]
    gath[n_atoms] = jnp.zeros((ROWS, LANES), jnp.bfloat16)

    pl.semaphore_wait(barrier, na - 1 + ne - 1)

    def send(d, _):
        pltpu.make_async_remote_copy(
            src_ref=gath.at[my_rows],
            dst_ref=gath.at[my_rows],
            send_sem=ag_send,
            recv_sem=ag_recv,
            device_id=(e, lax.rem(me + d, na)),
            device_id_type=MESH,
        ).start()
        return 0

    lax.fori_loop(1, na, send, 0)

    ab = form_matrix()
    loads[1].wait()
    for t in range(ROWS):
        tabx[pl.ds(t, KTAB, stride=ROWS), :] = tab_ref[
            0, :, t * LANES : (t + 1) * LANES
        ].astype(jnp.float32)

    def put_forms(dst, first, lhs):
        forms = dot(lhs, ab).astype(jnp.bfloat16)
        for k in range(lhs.shape[0] // ROWS):
            for s in range(4):
                dst[first + k, s * ROWS : (s + 1) * ROWS, :] = forms[
                    k * ROWS : (k + 1) * ROWS, s * LANES : (s + 1) * LANES
                ]

    def table_forms(i, _):
        rows = tabx[pl.ds(pl.multiple_of(i * 128, 128), 128), :]
        put_forms(gform, i * 8, with_partner(rows))
        return 0

    lax.fori_loop(0, KTAB // 8, table_forms, 0)
    put_forms(own_form, 0, with_partner(own32))

    def form(ref, k):
        return ref[k]

    sel = start_matrix()
    start = [dot_nt(sel, form(own_form, z)) for z in range(adev)]
    wide[...] = jnp.zeros_like(wide)
    for z in range(adev):
        wide[z * L : (z + 1) * L, :FORM] = start[z].astype(jnp.bfloat16)
    start_all = wide[0 : adev * L, :]

    def table_times_start(i, _):
        for k in range(8):
            b = i * 8 + k
            term = dot_nt(start_all, form(gform, b))
            for z in range(adev):
                pbuf[z, b] = term[z * L : (z + 1) * L]
        return 0

    lax.fori_loop(0, KTAB // 8, table_times_start, 0)
    for z in range(adev):
        pbuf[z, KTAB] = jnp.zeros((L, FORM), jnp.float32)

    slots = NB * NB
    for copy in loads[2:]:
        copy.wait()
    for buf in (c1, near1, near2):
        buf[...] = jnp.zeros_like(buf)
    for z in range(adev):

        def first_coupled(n, _, z=z):
            b = link[z, n]
            for m in range(NB):
                a = link[z, b * NB + m]
                acc = None
                for j in range(NB):
                    at = a * NB + j
                    term = pbuf[z, jnp.minimum(pair[z, at] + link[z, at] * KTAB, KTAB)]
                    acc = term if acc is None else acc + term
                c1[pl.ds(pl.multiple_of((z * slots + n * NB + m) * L, L), L), :FORM] = acc.astype(
                    jnp.bfloat16
                )
            return 0

        lax.fori_loop(0, NB, first_coupled, 0)

    others = gath.at[pl.ds(0, (na - 1) * adev)]
    pltpu.make_async_copy(others, others, ag_recv).wait()
    pltpu.make_async_copy(others, others, ag_send).wait()

    def member(z, a):
        absent = jnp.maximum(a - size[z] + 1, 0)
        return jnp.minimum(atoms[z, a] + absent * n_atoms, n_atoms)

    def is_first(a):
        return 1.0 - jnp.minimum(a, 1).astype(jnp.float32)

    tform[n_atoms] = jnp.zeros((FORM, LANES), jnp.bfloat16)
    step = min(16, n_atoms)

    def all_forms(i, _):
        rows = gath[pl.ds(i * step, step)].reshape(step * ROWS, LANES)
        put_forms(tform, i * step, with_partner(rows.astype(jnp.float32)))
        return 0

    lax.fori_loop(0, n_atoms // step, all_forms, 0)

    zn = [(z, n) for z in range(adev) for n in range(NB)]
    slot = {(z, n): link[z, n] for z, n in zn}

    for i, (z, n) in enumerate(zn):
        for m in range(NB):
            a = link[z, slot[z, n] * NB + m]
            at = (i * NB + m) * L
            col = dot_nt(c1[at : at + L, :], form(tform, member(z, a)))
            col = col + is_first(a) * start[z]
            near1[i * L : (i + 1) * L, m * LANES : m * LANES + FORM] = col.astype(jnp.bfloat16)

    for i, (z, n) in enumerate(zn):
        g = jnp.concatenate(
            [form(gform, pair[z, slot[z, n] * NB + m]) for m in range(NB)], axis=1
        )
        coupled = dot_nt(near1[i * L : (i + 1) * L, :], g)
        wide[i * L : (i + 1) * L, :FORM] = coupled.astype(jnp.bfloat16)
    for i, (z, n) in enumerate(zn):
        b = slot[z, n]
        col = dot_nt(wide[i * L : (i + 1) * L, :], form(tform, member(z, b)))
        col = col + is_first(b) * start[z]
        near2[z * L : (z + 1) * L, n * LANES : n * LANES + FORM] = col.astype(jnp.bfloat16)

    for z in range(adev):
        g = jnp.concatenate([form(gform, pair[z, n]) for n in range(NB)], axis=1)
        coupled = dot_nt(near2[z * L : (z + 1) * L, :], g)
        wide[z * L : (z + 1) * L, :FORM] = coupled.astype(jnp.bfloat16)

    lane_group = iota2((ROWS, LANES), 1) >> 5
    w_re = w_ref[0, 0]
    w_im = w_ref[0, 1]
    mine = pl.multiple_of(e * blk, blk)
    for z in range(adev):
        coupled = wide[z * L : (z + 1) * L, :]
        diag = dot_nt(form(own_form, z), jnp.concatenate([coupled] * 4, axis=0))
        block = xf[z * ROWS : (z + 1) * ROWS, :]
        for s in range(4):
            block = block + jnp.where(lane_group == s, diag[s * ROWS : (s + 1) * ROWS, :], 0.0)
        re, im = block[:8], block[8:]
        arbuf[pl.ds(mine + z * ROWS, 8), :] = w_re * re - w_im * im
        arbuf[pl.ds(mine + z * ROWS + 8, 8), :] = w_re * im + w_im * re

    def share(d, _):
        pltpu.make_async_remote_copy(
            src_ref=arbuf.at[pl.ds(mine, blk)],
            dst_ref=arbuf.at[pl.ds(mine, blk)],
            send_sem=ar_send,
            recv_sem=ar_recv,
            device_id=(lax.rem(e + d, ne), me),
            device_id_type=MESH,
        ).start()
        return 0

    lax.fori_loop(1, ne, share, 0)
    rest = arbuf.at[pl.ds(0, (ne - 1) * blk)]
    pltpu.make_async_copy(rest, rest, ar_recv).wait()
    pltpu.make_async_copy(rest, rest, ar_send).wait()
    green = arbuf[0:blk, :]
    for i in range(1, ne):
        green = green + arbuf[i * blk : (i + 1) * blk, :]
    out_ref[...] = green


def body(t_mats, struct_table, zone_atoms, zone_size, pair_index, zone_link, weights, ne, na):
    adev = t_mats.shape[1]
    slots = NB * NB
    given = (t_mats, struct_table, zone_atoms, zone_size, pair_index, zone_link, weights)
    bf16, f32 = jnp.bfloat16, jnp.float32
    green = pl.pallas_call(
        functools.partial(kernel, ne, na, adev),
        out_shape=jax.ShapeDtypeStruct((adev * ROWS, LANES), f32),
        in_specs=[pl.BlockSpec(memory_space=pltpu.HBM)] * len(given),
        out_specs=pl.BlockSpec(memory_space=pltpu.VMEM),
        scratch_shapes=[
            *[pltpu.VMEM(a.shape, a.dtype) for a in given[:2]],
            *[pltpu.SMEM(a.shape, a.dtype) for a in given[2:]],
            pltpu.VMEM((adev * ROWS, LANES), f32),
            pltpu.VMEM((na * adev + 1, ROWS, LANES), bf16),
            pltpu.VMEM((KTAB * ROWS, LANES), f32),
            pltpu.VMEM((KTAB, FORM, LANES), bf16),
            pltpu.VMEM((adev, FORM, LANES), bf16),
            pltpu.VMEM((na * adev + 1, FORM, LANES), bf16),
            pltpu.VMEM((adev, KTAB + 1, L, FORM), f32),
            pltpu.VMEM((adev * slots * L, LANES), bf16),
            pltpu.VMEM((adev * NB * L, NB * LANES), bf16),
            pltpu.VMEM((adev * L, NB * LANES), bf16),
            pltpu.VMEM((adev * NB * L, LANES), bf16),
            pltpu.VMEM((ne * adev * ROWS, LANES), f32),
            pltpu.SemaphoreType.DMA((len(given),)),
            pltpu.SemaphoreType.DMA,
            pltpu.SemaphoreType.DMA,
            pltpu.SemaphoreType.DMA,
            pltpu.SemaphoreType.DMA,
        ],
        compiler_params=pltpu.CompilerParams(
            collective_id=0, has_side_effects=True, vmem_limit_bytes=32 * 1024 * 1024
        ),
    )(*[pltpu.with_memory_space_constraint(a, pltpu.HBM) for a in given])
    return green.reshape(adev, 2 * L * L)


def solution(mesh):
    ne, na = mesh.shape["energy"], mesh.shape["atom"]
    return jax.shard_map(
        functools.partial(body, ne=ne, na=na),
        mesh=mesh,
        in_specs=(
            P("energy", "atom", None),
            P("energy", None, None),
            P("atom", None),
            P("atom"),
            P("atom", None),
            P("atom", None),
            P("energy", None),
        ),
        out_specs=P("atom", None),
        check_vma=False,
    )
```

```python
import functools

import jax
import jax.numpy as jnp
from jax import lax
from jax.experimental import pallas as pl
from jax.experimental.pallas import tpu as pltpu
from jax.sharding import PartitionSpec as P

L = 32
Z = 64
NB = 6
KTAB = 64
ROWS = 16
LANES = 128
FORM = 64
MESH = pl.DeviceIdType.MESH
NT = (((1,), (1,)), ((), ()))


def iota2(shape, dim):
    return lax.broadcasted_iota(jnp.int32, shape, dim)


def dot_nt(a, b):
    return lax.dot_general(a, b, NT, preferred_element_type=jnp.float32)


def dot(a, b):
    return jnp.dot(a, b, preferred_element_type=jnp.float32)


def to_bf16_mask(cond):
    return jnp.where(cond, 1.0, 0.0).astype(jnp.bfloat16)


def form_matrix():
    i = iota2((256, 512), 0)
    j = iota2((256, 512), 1)
    h, s1, c = i >> 7, (i >> 5) & 3, i & 31
    s, l = j >> 7, j & 127
    return to_bf16_mask(
        (s1 == s) & (l < 64) & (((l >> 3) & 1) == h) & (((l & 7) * 4 + (l >> 4)) == c)
    )


def start_matrix():
    k = iota2((L, LANES), 0)
    l = iota2((L, LANES), 1)
    return to_bf16_mask(
        (l < FORM) & (((l >> 3) & 1) == 0) & (((l & 7) * 4 + (l >> 4)) == k)
    )


def partner(x):
    n = x.shape[0] // ROWS
    halves = x.reshape(n, 2, 8, LANES)
    return jnp.concatenate([-halves[:, 1:], halves[:, :1]], axis=1).reshape(n * ROWS, LANES)


def with_partner(x32):
    return jnp.concatenate(
        [x32.astype(jnp.bfloat16), partner(x32).astype(jnp.bfloat16)], axis=1
    )


def ring(d, n):
    return min(d % n, -d % n)


def grid_of(na):
    chips = na // 2
    nx = max(d for d in range(1, chips + 1) if chips % d == 0 and d * d <= chips)
    return nx, chips // nx


def kernel(
    ne, na, adev,
    t_hbm, tab_hbm, atoms_hbm, size_hbm, pair_hbm, link_hbm, w_hbm,
    out_ref,
    t_ref, tab_ref, atoms, size, pair, link, w_ref,
    xf, gath, tabx, gform, own_form, tform, pbuf, c1, near1, near2, wide, arbuf,
    in_sems, ag_send, ag_recv, ar_send, ar_recv,
):
    e = lax.axis_index("energy")
    me = lax.axis_index("atom")
    n_atoms = na * adev
    blk = adev * ROWS

    sources = (t_hbm, tab_hbm, link_hbm, pair_hbm, atoms_hbm, size_hbm, w_hbm)
    landed = (t_ref, tab_ref, link, pair, atoms, size, w_ref)
    loads = [
        pltpu.make_async_copy(src, dst, in_sems.at[i])
        for i, (src, dst) in enumerate(zip(sources, landed))
    ]
    for copy in loads:
        copy.start()

    nx, ny = grid_of(na)
    core = lax.rem(me, 2)
    chip = lax.div(me, 2)
    x, y = lax.div(chip, ny), lax.rem(chip, ny)
    hops = {
        (dx, dy): ring(dx, nx) + ring(dy, ny)
        for dx in range(nx)
        for dy in range(ny)
        if dx + dy > 0
    }
    offsets = sorted(hops, key=lambda o: -hops[o])
    split = max(hops.values()) // 2
    groups = [
        [o for o in offsets if hops[o] > split],
        [o for o in offsets if 1 < hops[o] <= split],
        [o for o in offsets if hops[o] == 1],
    ]
    slot_of = {o: i for i, o in enumerate([(0, 0)] + offsets)}
    n_slots = len(slot_of)

    def chip_at(o):
        return lax.rem(x + o[0], nx) * ny + lax.rem(y + o[1], ny)

    def device_at(o, other):
        return (e, chip_at(o) * 2 + (1 - core if other else core))

    sibling = device_at((0, 0), True)
    energies = sorted(range(1, ne), key=lambda d: -ring(d, ne))

    barrier = pltpu.get_barrier_semaphore()

    def greet(device):
        pl.semaphore_signal(barrier, inc=1, device_id=device, device_id_type=MESH)

    for d in energies:
        greet((lax.rem(e + d, ne), me))
    for o in offsets:
        greet(device_at(o, False))
        greet(device_at(o, True))
    greet(sibling)

    loads[0].wait()
    for t in range(ROWS):
        xf[pl.ds(t, adev, stride=ROWS), :] = t_ref[
            0, :, t * LANES : (t + 1) * LANES
        ].astype(jnp.float32)
    own32 = xf[...]
    own = own32.astype(jnp.bfloat16)
    mine_at = core * n_slots
    for z in range(adev):
        gath[mine_at, z] = own[z * ROWS : (z + 1) * ROWS]

    pl.semaphore_wait(barrier, na - 1 + ne - 1)

    def wait_blocks(count, sem):
        blocks = gath.at[pl.ds(0, count)]
        pltpu.make_async_copy(blocks, blocks, sem).wait()

    def send(o, other, sem):
        dst = core * n_slots + slot_of[-o[0] % nx, -o[1] % ny]
        pltpu.make_async_remote_copy(
            src_ref=gath.at[mine_at],
            dst_ref=gath.at[dst],
            send_sem=ag_send,
            recv_sem=sem,
            device_id=device_at(o, other),
            device_id_type=MESH,
        ).start()

    for i, group in enumerate(groups):
        for o in group:
            send(o, True, ag_recv.at[i])
            send(o, False, ag_recv.at[i])
    send((0, 0), True, ag_recv.at[len(groups)])

    ab = form_matrix()
    loads[1].wait()
    for t in range(ROWS):
        tabx[pl.ds(t, KTAB, stride=ROWS), :] = tab_ref[
            0, :, t * LANES : (t + 1) * LANES
        ].astype(jnp.float32)

    def put_forms(dst, first, lhs):
        forms = dot(lhs, ab).astype(jnp.bfloat16)
        for k in range(lhs.shape[0] // ROWS):
            for s in range(4):
                dst[first + k, s * ROWS : (s + 1) * ROWS, :] = forms[
                    k * ROWS : (k + 1) * ROWS, s * LANES : (s + 1) * LANES
                ]

    def table_forms(i, _):
        rows = tabx[pl.ds(pl.multiple_of(i * 128, 128), 128), :]
        put_forms(gform, i * 8, with_partner(rows))
        return 0

    lax.fori_loop(0, KTAB // 8, table_forms, 0, unroll=4)
    put_forms(own_form, 0, with_partner(own32))

    def form(ref, k):
        return ref[k]

    sel = start_matrix()
    start = [dot_nt(sel, form(own_form, z)) for z in range(adev)]
    wide[...] = jnp.zeros_like(wide)
    for z in range(adev):
        wide[z * L : (z + 1) * L, :FORM] = start[z].astype(jnp.bfloat16)
    start_all = wide[0 : adev * L, :]

    def table_times_start(i, _):
        for k in range(8):
            b = i * 8 + k
            term = dot_nt(start_all, form(gform, b))
            for z in range(adev):
                pbuf[z, b] = term[z * L : (z + 1) * L]
        return 0

    lax.fori_loop(0, KTAB // 8, table_times_start, 0, unroll=4)
    for z in range(adev):
        pbuf[z, KTAB] = jnp.zeros((L, FORM), jnp.float32)

    slots = NB * NB
    for copy in loads[2:]:
        copy.wait()
    for buf in (c1, near1, near2):
        buf[...] = jnp.zeros_like(buf)
    for z in range(adev):

        def first_coupled(n, _, z=z):
            b = link[z, n]
            for m in range(NB):
                a = link[z, b * NB + m]
                acc = None
                for j in range(NB):
                    at = a * NB + j
                    term = pbuf[z, jnp.minimum(pair[z, at] + link[z, at] * KTAB, KTAB)]
                    acc = term if acc is None else acc + term
                c1[pl.ds(pl.multiple_of((z * slots + n * NB + m) * L, L), L), :FORM] = acc.astype(
                    jnp.bfloat16
                )
            return 0

        lax.fori_loop(0, NB, first_coupled, 0, unroll=NB)

    tform[n_atoms] = jnp.zeros((FORM, LANES), jnp.bfloat16)

    def forms_of(blocks):
        for first in range(0, len(blocks), 8):
            some = blocks[first : first + 8]
            rows = jnp.concatenate(
                [
                    gath[(1 - core if other else core) * n_slots + slot_of[o]].reshape(
                        adev * ROWS, LANES
                    )
                    for o, other in some
                ],
                axis=0,
            )
            forms = dot(with_partner(rows.astype(jnp.float32)), ab).astype(jnp.bfloat16)
            for i, (o, other) in enumerate(some):
                owner = chip_at(o) * 2 + (1 - core if other else core)
                for k in range(adev):
                    at = (i * adev + k) * ROWS
                    for s in range(4):
                        tform[owner * adev + k, s * ROWS : (s + 1) * ROWS, :] = forms[
                            at : at + ROWS, s * LANES : (s + 1) * LANES
                        ]

    wait_blocks(1, ag_recv.at[len(groups)])
    forms_of([((0, 0), False), ((0, 0), True)])
    for i, group in reversed(list(enumerate(groups))):
        if group:
            wait_blocks(2 * len(group), ag_recv.at[i])
            forms_of([(o, other) for o in group for other in (False, True)])

    def member(z, a):
        absent = jnp.maximum(a - size[z] + 1, 0)
        return jnp.minimum(atoms[z, a] + absent * n_atoms, n_atoms)

    def is_first(a):
        return 1.0 - jnp.minimum(a, 1).astype(jnp.float32)

    zn = [(z, n) for z in range(adev) for n in range(NB)]
    slot = {(z, n): link[z, n] for z, n in zn}

    for i, (z, n) in enumerate(zn):
        for m in range(NB):
            a = link[z, slot[z, n] * NB + m]
            at = (i * NB + m) * L
            col = dot_nt(c1[at : at + L, :], form(tform, member(z, a)))
            col = col + is_first(a) * start[z]
            near1[i * L : (i + 1) * L, m * LANES : m * LANES + FORM] = col.astype(jnp.bfloat16)

    for i, (z, n) in enumerate(zn):
        g = jnp.concatenate(
            [form(gform, pair[z, slot[z, n] * NB + m]) for m in range(NB)], axis=1
        )
        coupled = dot_nt(near1[i * L : (i + 1) * L, :], g)
        wide[i * L : (i + 1) * L, :FORM] = coupled.astype(jnp.bfloat16)
    for i, (z, n) in enumerate(zn):
        b = slot[z, n]
        col = dot_nt(wide[i * L : (i + 1) * L, :], form(tform, member(z, b)))
        col = col + is_first(b) * start[z]
        near2[z * L : (z + 1) * L, n * LANES : n * LANES + FORM] = col.astype(jnp.bfloat16)

    for z in range(adev):
        g = jnp.concatenate([form(gform, pair[z, n]) for n in range(NB)], axis=1)
        coupled = dot_nt(near2[z * L : (z + 1) * L, :], g)
        wide[z * L : (z + 1) * L, :FORM] = coupled.astype(jnp.bfloat16)

    lane_group = iota2((ROWS, LANES), 1) >> 5
    w_re = w_ref[0, 0]
    w_im = w_ref[0, 1]
    mine = pl.multiple_of(e * blk, blk)
    for z in range(adev):
        coupled = wide[z * L : (z + 1) * L, :]
        diag = dot_nt(form(own_form, z), jnp.concatenate([coupled] * 4, axis=0))
        block = xf[z * ROWS : (z + 1) * ROWS, :]
        for s in range(4):
            block = block + jnp.where(lane_group == s, diag[s * ROWS : (s + 1) * ROWS, :], 0.0)
        re, im = block[:8], block[8:]
        arbuf[pl.ds(mine + z * ROWS, 8), :] = w_re * re - w_im * im
        arbuf[pl.ds(mine + z * ROWS + 8, 8), :] = w_re * im + w_im * re

    for d in energies:
        pltpu.make_async_remote_copy(
            src_ref=arbuf.at[pl.ds(mine, blk)],
            dst_ref=arbuf.at[pl.ds(mine, blk)],
            send_sem=ar_send,
            recv_sem=ar_recv,
            device_id=(lax.rem(e + d, ne), me),
            device_id_type=MESH,
        ).start()
    rest = arbuf.at[pl.ds(0, (ne - 1) * blk)]
    pltpu.make_async_copy(rest, rest, ar_recv).wait()
    pltpu.make_async_copy(rest, rest, ar_send).wait()
    green = arbuf[0:blk, :]
    for i in range(1, ne):
        green = green + arbuf[i * blk : (i + 1) * blk, :]
    out_ref[...] = green
    wait_blocks(na - 1, ag_send)


def body(t_mats, struct_table, zone_atoms, zone_size, pair_index, zone_link, weights, ne, na):
    adev = t_mats.shape[1]
    slots = NB * NB
    given = (t_mats, struct_table, zone_atoms, zone_size, pair_index, zone_link, weights)
    bf16, f32 = jnp.bfloat16, jnp.float32
    green = pl.pallas_call(
        functools.partial(kernel, ne, na, adev),
        out_shape=jax.ShapeDtypeStruct((adev * ROWS, LANES), f32),
        in_specs=[pl.BlockSpec(memory_space=pltpu.HBM)] * len(given),
        out_specs=pl.BlockSpec(memory_space=pltpu.VMEM),
        scratch_shapes=[
            *[pltpu.VMEM(a.shape, a.dtype) for a in given[:2]],
            *[pltpu.SMEM(a.shape, a.dtype) for a in given[2:]],
            pltpu.VMEM((adev * ROWS, LANES), f32),
            pltpu.VMEM((na, adev, ROWS, LANES), bf16),
            pltpu.VMEM((KTAB * ROWS, LANES), f32),
            pltpu.VMEM((KTAB, FORM, LANES), bf16),
            pltpu.VMEM((adev, FORM, LANES), bf16),
            pltpu.VMEM((na * adev + 1, FORM, LANES), bf16),
            pltpu.VMEM((adev, KTAB + 1, L, FORM), f32),
            pltpu.VMEM((adev * slots * L, LANES), bf16),
            pltpu.VMEM((adev * NB * L, NB * LANES), bf16),
            pltpu.VMEM((adev * L, NB * LANES), bf16),
            pltpu.VMEM((adev * NB * L, LANES), bf16),
            pltpu.VMEM((ne * adev * ROWS, LANES), f32),
            pltpu.SemaphoreType.DMA((len(given),)),
            pltpu.SemaphoreType.DMA,
            pltpu.SemaphoreType.DMA((4,)),
            pltpu.SemaphoreType.DMA,
            pltpu.SemaphoreType.DMA,
        ],
        compiler_params=pltpu.CompilerParams(
            collective_id=0, has_side_effects=True, vmem_limit_bytes=32 * 1024 * 1024
        ),
    )(*[pltpu.with_memory_space_constraint(a, pltpu.HBM) for a in given])
    return green.reshape(adev, 2 * L * L)


def solution(mesh):
    ne, na = mesh.shape["energy"], mesh.shape["atom"]
    return jax.shard_map(
        functools.partial(body, ne=ne, na=na),
        mesh=mesh,
        in_specs=(
            P("energy", "atom", None),
            P("energy", None, None),
            P("atom", None),
            P("atom"),
            P("atom", None),
            P("atom", None),
            P("energy", None),
        ),
        out_specs=P("atom", None),
        check_vma=False,
    )
```

```python
import functools

import jax
import jax.numpy as jnp
from jax import lax
from jax.experimental import pallas as pl
from jax.experimental.pallas import tpu as pltpu
from jax.sharding import PartitionSpec as P

L = 32
Z = 64
NB = 6
KTAB = 64
ROWS = 16
LANES = 128
FORM = 64
MESH = pl.DeviceIdType.MESH
NT = (((1,), (1,)), ((), ()))


def iota2(shape, dim):
    return lax.broadcasted_iota(jnp.int32, shape, dim)


def dot_nt(a, b):
    return lax.dot_general(a, b, NT, preferred_element_type=jnp.float32)


def dot(a, b):
    return jnp.dot(a, b, preferred_element_type=jnp.float32)


def to_bf16_mask(cond):
    return jnp.where(cond, 1.0, 0.0).astype(jnp.bfloat16)


def form_matrix():
    i = iota2((256, 512), 0)
    j = iota2((256, 512), 1)
    h, s1, c = i >> 7, (i >> 5) & 3, i & 31
    s, l = j >> 7, j & 63
    return to_bf16_mask(
        (s1 == s) & (((l >> 3) & 1) == h) & (((l & 7) * 4 + (l >> 4)) == c)
    )


def start_matrix():
    k = iota2((L, LANES), 0)
    l = iota2((L, LANES), 1)
    return to_bf16_mask(
        (l < FORM) & (((l >> 3) & 1) == 0) & (((l & 7) * 4 + (l >> 4)) == k)
    )


def partner(x):
    n = x.shape[0] // ROWS
    halves = x.reshape(n, 2, 8, LANES)
    return jnp.concatenate([-halves[:, 1:], halves[:, :1]], axis=1).reshape(n * ROWS, LANES)


def with_partner(x32):
    return jnp.concatenate(
        [x32.astype(jnp.bfloat16), partner(x32).astype(jnp.bfloat16)], axis=1
    )


def ring(d, n):
    return min(d % n, -d % n)


def grid_of(na):
    chips = na // 2
    nx = max(d for d in range(1, chips + 1) if chips % d == 0 and d * d <= chips)
    return nx, chips // nx


def kernel(
    ne, na, adev,
    t_hbm, tab_hbm, atoms_hbm, size_hbm, pair_hbm, link_hbm, w_hbm,
    out_ref,
    t_ref, tab_ref, size, w_ref, *scratch,
):
    link, pair, atoms = (scratch[i * adev : (i + 1) * adev] for i in range(3))
    (
        t_at, g_at, first_at,
        xf, gath, tabx, gform, own_form, tform, pbuf, start4, c1, near1, c2, near2, c3, arbuf,
        in_sems, ag_send, ag_recv, ar_send, ar_recv,
    ) = scratch[3 * adev :]
    e = lax.axis_index("energy")
    me = lax.axis_index("atom")
    n_atoms = na * adev
    blk = adev * ROWS

    sources = [t_hbm, tab_hbm, size_hbm, w_hbm]
    landed = [t_ref, tab_ref, size, w_ref]
    for z in range(adev):
        sources += [link_hbm.at[z], pair_hbm.at[z], atoms_hbm.at[z]]
        landed += [link[z], pair[z], atoms[z]]
    loads = [
        pltpu.make_async_copy(src, dst, in_sems.at[i])
        for i, (src, dst) in enumerate(zip(sources, landed))
    ]
    for copy in loads:
        copy.start()

    nx, ny = grid_of(na)
    core = lax.rem(me, 2)
    chip = lax.div(me, 2)
    x, y = lax.div(chip, ny), lax.rem(chip, ny)
    hops = {
        (dx, dy): ring(dx, nx) + ring(dy, ny)
        for dx in range(nx)
        for dy in range(ny)
        if dx + dy > 0
    }
    offsets = sorted(hops, key=lambda o: -hops[o])
    groups = [
        [o for o in offsets if hops[o] == h] for h in range(max(hops.values()), 0, -1)
    ]
    slot_of = {o: i for i, o in enumerate([(0, 0)] + offsets)}
    n_slots = len(slot_of)

    def chip_at(o):
        return lax.rem(x + o[0], nx) * ny + lax.rem(y + o[1], ny)

    def device_at(o, other):
        return (e, chip_at(o) * 2 + (1 - core if other else core))

    sibling = device_at((0, 0), True)
    energies = sorted(range(1, ne), key=lambda d: -ring(d, ne))

    barrier = pltpu.get_barrier_semaphore()

    def greet(device):
        pl.semaphore_signal(barrier, inc=1, device_id=device, device_id_type=MESH)

    for d in energies:
        greet((lax.rem(e + d, ne), me))
    for o in offsets:
        greet(device_at(o, False))
        greet(device_at(o, True))
    greet(sibling)

    loads[0].wait()
    for t in range(ROWS):
        xf[pl.ds(t, adev, stride=ROWS), :] = t_ref[
            0, :, t * LANES : (t + 1) * LANES
        ].astype(jnp.float32)
    own32 = xf[...]
    own = own32.astype(jnp.bfloat16)
    mine_at = core * n_slots
    for z in range(adev):
        gath[mine_at, z] = own[z * ROWS : (z + 1) * ROWS]

    pl.semaphore_wait(barrier, na - 1 + ne - 1)

    def wait_blocks(count, sem):
        blocks = gath.at[pl.ds(0, count)]
        pltpu.make_async_copy(blocks, blocks, sem).wait()

    def send(o, other, sem):
        dst = core * n_slots + slot_of[-o[0] % nx, -o[1] % ny]
        pltpu.make_async_remote_copy(
            src_ref=gath.at[mine_at],
            dst_ref=gath.at[dst],
            send_sem=ag_send,
            recv_sem=sem,
            device_id=device_at(o, other),
            device_id_type=MESH,
        ).start()

    for i, group in enumerate(groups):
        for o in group:
            send(o, True, ag_recv.at[i])
            send(o, False, ag_recv.at[i])
    send((0, 0), True, ag_recv.at[len(groups)])

    ab = form_matrix()
    loads[1].wait()
    for t in range(ROWS):
        tabx[pl.ds(t, KTAB, stride=ROWS), :] = tab_ref[
            0, :, t * LANES : (t + 1) * LANES
        ].astype(jnp.float32)

    def put_forms(dst, first, lhs):
        forms = dot(lhs, ab).astype(jnp.bfloat16)
        for k in range(lhs.shape[0] // ROWS):
            for s in range(4):
                dst[first + k, s * ROWS : (s + 1) * ROWS, :] = forms[
                    k * ROWS : (k + 1) * ROWS, s * LANES : (s + 1) * LANES
                ]

    def table_forms(i, _):
        rows = tabx[pl.ds(pl.multiple_of(i * 128, 128), 128), :]
        put_forms(gform, i * 8, with_partner(rows))
        return 0

    lax.fori_loop(0, KTAB // 8, table_forms, 0, unroll=4)
    put_forms(own_form, 0, with_partner(own32))

    def form(ref, k):
        return ref[k]

    sel = start_matrix()
    start = [dot_nt(sel, form(own_form, z)) for z in range(adev)]
    for buf in (start4, c1, c2, c3):
        buf[...] = jnp.zeros_like(buf)
    for q in range(4):
        for z in range(adev):
            at = (q * adev + z) * L
            start4[at : at + L, q * FORM : (q + 1) * FORM] = start[z].astype(jnp.bfloat16)

    low = iota2((FORM, LANES), 1) < FORM

    def side_by_side(forms):
        return jnp.concatenate(
            [
                jnp.where(low, forms[i], forms[i + 1])
                for i in range(0, len(forms), 2)
            ],
            axis=1,
        )

    def table_times_start(i, _):
        for j in range(2):
            k = i * 8 + j * 4
            terms = dot_nt(
                start4[...], side_by_side([form(gform, k + q) for q in range(4)])
            )
            for q in range(4):
                for z in range(adev):
                    at = (q * adev + z) * L
                    pbuf[z, k + q] = terms[at : at + L]
        return 0

    lax.fori_loop(0, KTAB // 8, table_times_start, 0, unroll=4)
    for z in range(adev):
        pbuf[z, KTAB] = jnp.zeros((L, FORM), jnp.float32)

    for copy in loads[2:]:
        copy.wait()
    wanted = [(z, n, m) for z in range(adev) for n in range(NB) for m in range(NB)]
    zn = [(z, n) for z in range(adev) for n in range(NB)]

    def block(i):
        row = (i // 4) * 4 * L + (i % 4) * L
        return slice(row, row + L), slice((i % 4) * FORM, (i % 4 + 1) * FORM)

    def member(z, a):
        absent = jnp.maximum(a - size[z] + 1, 0)
        return jnp.minimum(atoms[z][a] + absent * n_atoms, n_atoms)

    def note(i, z, a, at):
        t_at[i] = member(z, a)
        g_at[i] = pair[z][at]
        first_at[i] = 1.0 - jnp.minimum(a, 1).astype(jnp.float32)

    for i, (z, n, m) in enumerate(wanted):
        link_at = link[z][n] * NB + m
        a = link[z][link_at]
        note(i, z, a, link_at)
        acc = None
        for j in range(NB):
            at = a * NB + j
            term = pbuf[z, jnp.minimum(pair[z][at] + link[z][at] * KTAB, KTAB)]
            acc = term if acc is None else acc + term
        c1[block(i)] = acc.astype(jnp.bfloat16)
    inner = len(wanted)
    for i, (z, n) in enumerate(zn):
        note(inner + i, z, link[z][n], n)

    tform[n_atoms] = jnp.zeros((FORM, LANES), jnp.bfloat16)

    def forms_of(blocks):
        for first in range(0, len(blocks), 8):
            some = blocks[first : first + 8]
            rows = jnp.concatenate(
                [
                    gath[(1 - core if other else core) * n_slots + slot_of[o]].reshape(
                        adev * ROWS, LANES
                    )
                    for o, other in some
                ],
                axis=0,
            )
            forms = dot(with_partner(rows.astype(jnp.float32)), ab).astype(jnp.bfloat16)
            for i, (o, other) in enumerate(some):
                owner = chip_at(o) * 2 + (1 - core if other else core)
                for k in range(adev):
                    at = (i * adev + k) * ROWS
                    for s in range(4):
                        tform[owner * adev + k, s * ROWS : (s + 1) * ROWS, :] = forms[
                            at : at + ROWS, s * LANES : (s + 1) * LANES
                        ]

    wait_blocks(1, ag_recv.at[len(groups)])
    forms_of([((0, 0), False), ((0, 0), True)])
    for i, group in enumerate(groups):
        if group:
            wait_blocks(2 * len(group), ag_recv.at[i])
            forms_of([(o, other) for o in group for other in (False, True)])

    def columns(states, first, base):
        at = base + first
        forms = side_by_side([form(tform, t_at[at + q]) for q in range(4)])
        cols = dot_nt(states[first * L : (first + 4) * L, :], forms)
        return [(cols[q * L : (q + 1) * L], first_at[at + q]) for q in range(4)]

    for first in range(0, inner, 4):
        for q, (col, here) in enumerate(columns(c1, first, 0)):
            z, n, m = wanted[first + q]
            at = (z * NB + n) * L
            near1[at : at + L, m * FORM : (m + 1) * FORM] = (col + here * start[z]).astype(
                jnp.bfloat16
            )

    for i in range(len(zn)):
        g = side_by_side([form(gform, g_at[i * NB + m]) for m in range(NB)])
        c2[block(i)] = dot_nt(near1[i * L : (i + 1) * L, :], g).astype(jnp.bfloat16)
    for first in range(0, len(zn), 4):
        for q, (col, here) in enumerate(columns(c2, first, inner)):
            z, n = zn[first + q]
            near2[z * L : (z + 1) * L, n * FORM : (n + 1) * FORM] = (
                col + here * start[z]
            ).astype(jnp.bfloat16)

    for z in range(adev):
        g = side_by_side([form(gform, g_at[inner + z * NB + n]) for n in range(NB)])
        c3[z * L : (z + 1) * L, :FORM] = dot_nt(near2[z * L : (z + 1) * L, :], g).astype(
            jnp.bfloat16
        )

    lane_group = iota2((ROWS, LANES), 1) >> 5
    w_re = w_ref[0, 0]
    w_im = w_ref[0, 1]
    mine = pl.multiple_of(e * blk, blk)
    for z in range(adev):
        coupled = c3[z * L : (z + 1) * L, :]
        diag = dot_nt(form(own_form, z), jnp.concatenate([coupled] * 4, axis=0))
        diagonal = xf[z * ROWS : (z + 1) * ROWS, :]
        for s in range(4):
            diagonal = diagonal + jnp.where(lane_group == s, diag[s * ROWS : (s + 1) * ROWS, :], 0.0)
        re, im = diagonal[:8], diagonal[8:]
        arbuf[pl.ds(mine + z * ROWS, 8), :] = w_re * re - w_im * im
        arbuf[pl.ds(mine + z * ROWS + 8, 8), :] = w_re * im + w_im * re

    for d in energies:
        pltpu.make_async_remote_copy(
            src_ref=arbuf.at[pl.ds(mine, blk)],
            dst_ref=arbuf.at[pl.ds(mine, blk)],
            send_sem=ar_send,
            recv_sem=ar_recv,
            device_id=(lax.rem(e + d, ne), me),
            device_id_type=MESH,
        ).start()
    rest = arbuf.at[pl.ds(0, (ne - 1) * blk)]
    pltpu.make_async_copy(rest, rest, ar_recv).wait()
    pltpu.make_async_copy(rest, rest, ar_send).wait()
    green = arbuf[0:blk, :]
    for i in range(1, ne):
        green = green + arbuf[i * blk : (i + 1) * blk, :]
    out_ref[...] = green
    wait_blocks(na - 1, ag_send)


def body(t_mats, struct_table, zone_atoms, zone_size, pair_index, zone_link, weights, ne, na):
    adev = t_mats.shape[1]
    given = (t_mats, struct_table, zone_atoms, zone_size, pair_index, zone_link, weights)
    bf16, f32 = jnp.bfloat16, jnp.float32
    green = pl.pallas_call(
        functools.partial(kernel, ne, na, adev),
        out_shape=jax.ShapeDtypeStruct((adev * ROWS, LANES), f32),
        in_specs=[pl.BlockSpec(memory_space=pltpu.HBM)] * len(given),
        out_specs=pl.BlockSpec(memory_space=pltpu.VMEM),
        scratch_shapes=[
            *[pltpu.VMEM(a.shape, a.dtype) for a in given[:2]],
            pltpu.SMEM(zone_size.shape, zone_size.dtype),
            pltpu.SMEM(weights.shape, weights.dtype),
            *[pltpu.SMEM((Z * NB,), jnp.int32)] * (2 * adev),
            *[pltpu.SMEM((Z,), jnp.int32)] * adev,
            pltpu.SMEM((adev * NB * (NB + 1),), jnp.int32),
            pltpu.SMEM((adev * NB * (NB + 1),), jnp.int32),
            pltpu.SMEM((adev * NB * (NB + 1),), f32),
            pltpu.VMEM((adev * ROWS, LANES), f32),
            pltpu.VMEM((na, adev, ROWS, LANES), bf16),
            pltpu.VMEM((KTAB * ROWS, LANES), f32),
            pltpu.VMEM((KTAB, FORM, LANES), bf16),
            pltpu.VMEM((adev, FORM, LANES), bf16),
            pltpu.VMEM((na * adev + 1, FORM, LANES), bf16),
            pltpu.VMEM((adev, KTAB + 1, L, FORM), f32),
            pltpu.VMEM((4 * adev * L, 4 * FORM), bf16),
            pltpu.VMEM((adev * NB * NB * L, 4 * FORM), bf16),
            pltpu.VMEM((adev * NB * L, NB * FORM), bf16),
            pltpu.VMEM((adev * NB * L, 4 * FORM), bf16),
            pltpu.VMEM((adev * L, NB * FORM), bf16),
            pltpu.VMEM((adev * L, LANES), bf16),
            pltpu.VMEM((ne * adev * ROWS, LANES), f32),
            pltpu.SemaphoreType.DMA((4 + 3 * adev,)),
            pltpu.SemaphoreType.DMA,
            pltpu.SemaphoreType.DMA((8,)),
            pltpu.SemaphoreType.DMA,
            pltpu.SemaphoreType.DMA,
        ],
        compiler_params=pltpu.CompilerParams(
            collective_id=0, has_side_effects=True, vmem_limit_bytes=32 * 1024 * 1024
        ),
    )(*[pltpu.with_memory_space_constraint(a, pltpu.HBM) for a in given])
    return green.reshape(adev, 2 * L * L)


def solution(mesh):
    ne, na = mesh.shape["energy"], mesh.shape["atom"]
    return jax.shard_map(
        functools.partial(body, ne=ne, na=na),
        mesh=mesh,
        in_specs=(
            P("energy", "atom", None),
            P("energy", None, None),
            P("atom", None),
            P("atom"),
            P("atom", None),
            P("atom", None),
            P("energy", None),
        ),
        out_specs=P("atom", None),
        check_vma=False,
    )
```
